256 devices in a mesh: rep: 8 (over z), shard: 32 (over x, y, core).
Axes of the slice: x: 4, y: 4, z: 8, core: 2. Of those that a mesh axis runs over, the one named last changes fastest.
Arguments:
- acts: bfloat16 [131072, 2048], P(('rep', 'shard')), may hold values from -6 to 6
- cotangent: bfloat16 [131072, 5120], P(('rep', 'shard')), may hold values from -0.046875 to 0.046875
- error_prev: float32 [8, 2048, 5120], P('rep', 'shard'), may hold values from -6 to 6
- q_prev: float32 [5120, 64], replicated, may hold values from -6 to 6
Outputs:
- update: bfloat16 [2048, 5120], P('shard')
- error_next: float32 [8, 2048, 5120], P('rep', 'shard')
- q_next: float32 [5120, 64], replicated
The draws below stay inside these ranges and needn't reach their ends.
All inputs are finite; a program needn't handle non-finite values.
Results may differ from the reference program's by a relative error of at most 0.025.
Values may be sent and summed in bfloat16 or wider, within the bound.
No kernel may reach another device: no remote copies, remote signals or barrier semaphores. Data moves between devices by JAX's collectives and lax.ppermute only.
A program may use at most 128 MiB of HBM per device.

```python
import jax
import jax.numpy as jnp
from jax import lax

D = 2048
FFW = 5120
RANK = 64
TOK_DEV = 512
TOKENS = 131072
N_REP = 8
N_SHARD = 32


def block_scale(rng, extent, cuts, low, high):
    level, own = 1.0, jax.random.fold_in(rng, 6)
    for position, shards_of in cuts:
        draws = jnp.exp(jax.random.uniform(jax.random.fold_in(own, position), (shards_of,), jnp.float32, low / len(cuts), high / len(cuts)))
        level = level * jnp.repeat(draws, extent[position] // shards_of).reshape([-1 if axis == position else 1 for axis in range(len(extent))])
    return level


def noise(own_key, shape, scale, bound, pieces=(), kind=jnp.bfloat16):
    level = block_scale(own_key, shape, pieces, -0.22, 0.18) if pieces else 1.0
    array = jax.random.normal(own_key, shape, jnp.float32) * scale * level
    return jnp.minimum(jnp.maximum(array, -bound), bound).astype(kind)


def setup_inputs(seed: int = 0) -> dict:
    keys = jax.random.split(jax.random.key(seed), 5)
    acts = noise(keys[0], (TOKENS, D), 1.0, 6.0, ((0, 256),))
    cotangent = noise(keys[1], (TOKENS, FFW), (TOK_DEV * N_SHARD) ** -0.5, 0.046875, ((0, 256),))
    error_prev = noise(keys[2], (N_REP, D, FFW), 1.0, 6.0, ((0, 8), (1, 32)), jnp.float32)
    q_prev = noise(keys[3], (FFW, RANK), 1.0, 6.0, (), jnp.float32)
    return dict(acts=acts, cotangent=cotangent, error_prev=error_prev, q_prev=q_prev)


def reference(acts, cotangent, error_prev, q_prev):
    hi = lax.Precision.HIGHEST
    xs = acts.reshape(N_REP, N_SHARD, TOK_DEV, D)
    ys = cotangent.reshape(N_REP, N_SHARD, TOK_DEV, FFW)

    def replica_grad(pair):
        x_rep, y_rep = pair

        def add_block(total, block):
            x_blk, y_blk = block
            partial_term = lax.dot_general(x_blk.astype(jnp.float32), y_blk.astype(jnp.float32), (((0,), (0,)), ((), ())), preferred_element_type=jnp.float32)
            rounded = lax.optimization_barrier(partial_term.astype(jnp.bfloat16))
            return (total + rounded.astype(jnp.float32), None)
        total, unused = lax.scan(add_block, jnp.zeros((D, FFW), jnp.float32), (x_rep, y_rep))
        return total
    grads = lax.map(replica_grad, (xs, ys))
    mixed = grads + error_prev
    p_sum = jnp.zeros((D, RANK), jnp.float32)
    for index in range(N_REP):
        p_sum = p_sum + jnp.dot(mixed[index], q_prev, precision=hi)
    gram = jnp.dot(p_sum.T, p_sum, precision=hi)
    lower = jnp.linalg.cholesky(gram)
    p_hat = lax.linalg.triangular_solve(lower, p_sum, left_side=False, lower=True, transpose_a=True)
    q_sum = jnp.zeros((FFW, RANK), jnp.float32)
    for index in range(N_REP):
        q_sum = q_sum + jnp.dot(mixed[index].T, p_hat, precision=hi)
    q_next = q_sum / N_REP
    full_update = jnp.dot(p_hat, q_next.T, precision=hi)
    error_next = mixed - full_update[None]
    return (full_update.astype(jnp.bfloat16), error_next, q_next)
```

```python
import jax
import jax.numpy as jnp
from jax import lax
from jax.experimental import pallas as pl
from jax.experimental.pallas import tpu as pltpu
from jax.sharding import Mesh, PartitionSpec as P

HI = lax.Precision.HIGHEST
SHARD = ("x", "y", "c")
f32 = jnp.float32
bf16 = jnp.bfloat16


def halves(a, axis):
    top = a.astype(bf16)
    rest = (a - top.astype(f32)).astype(bf16)
    return jnp.concatenate([top, rest], axis)


def fold(a, axis):
    one, two = jnp.split(a, 2, axis)
    return one + two


def pair_product_body(core, a0, a1, y0, y1, out):
    del core
    left0 = a0[...].T
    left1 = a1[...].T
    wide = 512
    for start in range(0, out.shape[1], wide):
        cols = slice(start, start + wide)
        total = jnp.dot(left0, y0[:, cols], preferred_element_type=f32)
        total += jnp.dot(left1, y1[:, cols], preferred_element_type=f32)
        out[:, cols] = total.astype(out.dtype)


def pair_product(core, a0, a1, y0, y1):
    tokens, rows = a0.shape
    cols = y1.shape[1]
    tile = 256
    return pl.pallas_call(
        pair_product_body,
        out_shape=jax.ShapeDtypeStruct((rows, cols), bf16),
        grid_spec=pltpu.PrefetchScalarGridSpec(
            num_scalar_prefetch=1,
            grid=(rows // tile,),
            in_specs=[
                pl.BlockSpec((tokens, tile), lambda i, core: (0, i)),
                pl.BlockSpec((tokens, tile), lambda i, core: (0, i)),
                pl.BlockSpec((tokens, cols), lambda i, core: (0, core[0])),
                pl.BlockSpec((tokens, cols), lambda i, core: (0, 0)),
            ],
            out_specs=pl.BlockSpec((tile, cols), lambda i, core: (i, 0)),
        ),
        compiler_params=pltpu.CompilerParams(vmem_limit_bytes=40 * 2**20),
        cost_estimate=pl.CostEstimate(
            flops=4 * tokens * rows * cols, bytes_accessed=20_000_000, transcendentals=0
        ),
    )(core, a0, a1, y0, y1)


def exchange(a, axes):
    return lax.all_to_all(a, axes, 0, 0, tiled=True)


def gather(a, axes, count):
    return exchange(jnp.broadcast_to(a[None], (count,) + a.shape), axes)


def on_device(acts, cot, error_prev, q_prev):
    c = lax.axis_index("c")
    n_rep = lax.axis_size("z")
    n_shard = lax.axis_size("x") * lax.axis_size("y") * lax.axis_size("c")
    swap = [(0, 1), (1, 0)]
    err = error_prev[0]
    own, ffw = err.shape
    rank = q_prev.shape[1]
    dim = acts.shape[1]
    half = ffw // 2

    acts_other = lax.ppermute(acts, "c", swap)
    cot_other = lax.ppermute(lax.dynamic_slice_in_dim(cot, (1 - c) * half, half, 1), "c", swap)

    t = fold(jnp.dot(cot, halves(q_prev, 1), preferred_element_type=f32), 1)
    p_part = fold(
        lax.dot_general(acts, halves(t, 1), (((0,), (0,)), ((), ())), preferred_element_type=f32), 1
    )
    p_err = jnp.dot(err, q_prev, precision=HI)

    partial = pair_product(c.astype(jnp.int32)[None], acts, acts_other, cot, cot_other)
    partial, p_part = lax.optimization_barrier((partial, p_part))
    grad_half = lax.psum_scatter(partial, ("x", "y"), scatter_dimension=0, tiled=True)

    def pack(a):
        return jnp.concatenate([a[..., : own // 2, :], a[..., own // 2 :, :]], -1)

    def unpack(a):
        return jnp.concatenate([a[..., :rank], a[..., rank:]], -2)

    p_own = exchange(pack(p_part.reshape(n_shard, own, rank)), SHARD).sum(0) + pack(p_err)
    p_own = gather(p_own, "z", n_rep).sum(0)
    p = unpack(gather(p_own, SHARD, n_shard)).reshape(dim, rank)
    gram = lax.dot_general(p, p, (((0,), (0,)), ((), ())), precision=HI)
    lower = jnp.linalg.cholesky(gram)
    inverse = lax.linalg.triangular_solve(lower, jnp.eye(rank, dtype=f32), left_side=True, lower=True)
    p_hat = lax.dot_general(p, inverse, (((1,), (1,)), ((), ())), precision=HI)
    p_hat_own = lax.dot_general(unpack(p_own), inverse, (((1,), (1,)), ((), ())), precision=HI)

    w = fold(jnp.dot(acts, halves(p_hat, 1), preferred_element_type=f32), 1)
    q_part = fold(
        lax.dot_general(halves(w, 1), cot, (((0,), (0,)), ((), ())), preferred_element_type=f32), 0
    )
    q_part += lax.dot_general(p_hat_own, err, (((0,), (0,)), ((), ())), precision=HI)
    high, wide = 16, rank * ffw // n_shard // 16
    blocks = q_part.astype(bf16).reshape(rank // high, high, ffw // wide, wide)
    blocks = blocks.transpose(0, 2, 1, 3).reshape(n_shard, high, wide)
    q_own = exchange(blocks, SHARD).astype(f32).sum(0)
    q_own = gather(q_own, "z", n_rep).sum(0) / n_rep
    q_all = gather(q_own.astype(bf16), SHARD, n_shard)
    q_t = q_all.reshape(rank // high, ffw // wide, high, wide).transpose(0, 2, 1, 3)
    q_t = q_t.reshape(rank, ffw).astype(f32)

    update = jnp.dot(p_hat_own, q_t, precision=HI)
    mine = lax.dynamic_slice_in_dim(grad_half, c * own, own, 0)
    theirs = lax.dynamic_slice_in_dim(grad_half, (1 - c) * own, own, 0)
    theirs = lax.ppermute(theirs, "c", swap)
    grad = jnp.where(
        c == 0,
        jnp.concatenate([mine, theirs], 1),
        jnp.concatenate([theirs, mine], 1),
    )
    error_next = (grad.astype(f32) + err - update)[None]
    return update.astype(bf16), error_next, q_t.T


def solution(mesh):
    reps, shards = mesh.devices.shape
    side = int((shards // 2) ** 0.5)
    grid = Mesh(mesh.devices.reshape(reps, side, side, 2), ("z",) + SHARD)
    every = ("z",) + SHARD
    return jax.shard_map(
        on_device,
        mesh=grid,
        in_specs=(P(every, None), P(every, None), P("z", SHARD, None), P()),
        out_specs=(P(SHARD, None), P("z", SHARD, None), P()),
        check_vma=False,
    )
```

```python
import functools

import jax
import jax.numpy as jnp
from jax import lax
from jax.experimental import pallas as pl
from jax.experimental.pallas import tpu as pltpu
from jax.sharding import Mesh, PartitionSpec as P

HI = lax.Precision.HIGHEST
SHARD = ("x", "y", "c")
f32 = jnp.float32
bf16 = jnp.bfloat16
VMEM = pl.BlockSpec(memory_space=pltpu.VMEM)
SMEM = pl.BlockSpec(memory_space=pltpu.SMEM)
NT = (((1,), (1,)), ((), ()))


def terms(a, count):
    out = []
    for _ in range(count):
        top = a.astype(bf16)
        out.append(top)
        a = a - top.astype(f32)
    return out


def rows2(a):
    return jnp.concatenate(terms(a, 2), 0)


def fold(a):
    size = a.shape[0] // 2
    return a[:size] + a[size:]


def call(body, outs, ins, flops, name, scratch=(), limit=32):
    size = sum(o.size * o.dtype.itemsize for o in outs) + sum(a.size * a.dtype.itemsize for a, _ in ins)
    return pl.pallas_call(
        body,
        out_shape=outs,
        in_specs=[spec for _, spec in ins],
        out_specs=[VMEM] * len(outs),
        scratch_shapes=list(scratch),
        name=name,
        compiler_params=pltpu.CompilerParams(vmem_limit_bytes=limit * 2**20),
        cost_estimate=pl.CostEstimate(flops=flops, bytes_accessed=size, transcendentals=0),
    )(*[a for a, _ in ins])


def shape(dims, dtype):
    return jax.ShapeDtypeStruct(dims, dtype)


def left_body(meta, q_t, cot, acts, err, out, p_t):
    q2 = rows2(q_t[...])
    t = fold(lax.dot_general(q2, cot[...], NT, preferred_element_type=f32))
    p_t[...] = fold(jnp.dot(rows2(t), acts[...], preferred_element_type=f32))
    own = fold(lax.dot_general(q2, rows2(err[...]), NT, preferred_element_type=f32))
    rows = err.shape[0]
    own = own[:, :rows] + own[:, rows:]
    s = meta[1]
    zero = jnp.zeros_like(own)
    odd = (s % 2) == 1
    own = jnp.concatenate([jnp.where(odd, zero, own), jnp.where(odd, own, zero)], 1)
    at = pl.ds(pl.multiple_of((s // 2) * (2 * rows), 2 * rows), 2 * rows)
    p_t[:, at] += own
    _, high, wide = out.shape
    across = p_t.shape[1] // wide
    for block in range(out.shape[0]):
        g, l = divmod(block, across)
        out[block] = p_t[g * high : (g + 1) * high, l * wide : (l + 1) * wide]


def total_body(scale, part, out):
    total = part[0].astype(f32)
    for index in range(1, part.shape[0]):
        total += part[index].astype(f32)
    total = (total * scale).astype(out.dtype)
    for index in range(out.shape[0]):
        out[index] = total


def total(part, copies, dtype, name, scale=1.0):
    out = shape((copies,) + part.shape[1:], dtype)
    return call(functools.partial(total_body, scale), [out], [(part, VMEM)], part.size, name)[0]


def inverse_factor(gram):
    n = gram.shape[0]
    ident = (
        lax.broadcasted_iota(jnp.int32, (n, n), 0) == lax.broadcasted_iota(jnp.int32, (n, n), 1)
    ).astype(f32)
    work = jnp.concatenate([gram, ident], 1)
    index = lax.broadcasted_iota(jnp.int32, work.shape, 0)
    for k in range(n):
        row = jnp.broadcast_to(work[k : k + 1, :], work.shape)
        col = jnp.broadcast_to(work[:, k : k + 1], work.shape)
        pivot = jnp.broadcast_to(work[k : k + 1, k : k + 1], work.shape)
        root = lax.rsqrt(pivot)
        work = jnp.where(
            index > k, work - col * (row / pivot), jnp.where(index == k, row * root, work)
        )
    return work[:, n:]


def right_body(meta, parts, acts, cot, err, out, own_out, p_t):
    _, high, wide = parts.shape
    across = p_t.shape[1] // wide
    for block in range(parts.shape[0]):
        g, l = divmod(block, across)
        p_t[g * high : (g + 1) * high, l * wide : (l + 1) * wide] = parts[block]
    rank = p_t.shape[0]
    rows = err.shape[0]
    p = p_t[...]
    p3 = jnp.concatenate(terms(p, 3), 0)
    grams = lax.dot_general(p3, p3, NT, preferred_element_type=f32)
    gram = jnp.zeros((rank, rank), f32)
    for i in reversed(range(3)):
        for j in reversed(range(3)):
            gram += grams[i * rank : (i + 1) * rank, j * rank : (j + 1) * rank]
    inverse = inverse_factor(gram)
    p_hat = jnp.dot(inverse, p, precision=HI, preferred_element_type=f32)
    p_t[...] = p_hat
    w = fold(lax.dot_general(rows2(p_hat), acts[...], NT, preferred_element_type=f32))
    w2 = rows2(w)
    s = meta[1]
    both = p_t[:, pl.ds(pl.multiple_of((s // 2) * (2 * rows), 2 * rows), 2 * rows)]
    own = jnp.where((s % 2) == 1, both[:, rows:], both[:, :rows])
    own_out[...] = own
    own_top, own_rest = terms(own, 2)
    own3 = jnp.concatenate([own_top, own_rest, own_top], 1)
    _, high, wide = out.shape
    across = cot.shape[1] // wide
    for l in range(across):
        cols = slice(l * wide, (l + 1) * wide)
        err_top, err_rest = terms(err[:, cols], 2)
        err3 = jnp.concatenate([err_top, err_top, err_rest], 0)
        q = fold(jnp.dot(w2, cot[:, cols], preferred_element_type=f32))
        q += jnp.dot(own3, err3, preferred_element_type=f32)
        q = q.astype(out.dtype)
        for g in range(rank // high):
            out[g * across + l] = q[g * high : (g + 1) * high]


def last_body(meta, parts, own_t, mine, theirs, err, update, error_next, q_out):
    _, high, wide = parts.shape
    rank = own_t.shape[0]
    across = err.shape[1] // wide
    own_top, own_rest = terms(own_t[...].T, 2)
    own2 = jnp.concatenate([own_top, own_rest], 1)
    c = meta[0]
    for l in range(across):
        cols = slice(l * wide, (l + 1) * wide)
        q = jnp.concatenate([parts[g * across + l] for g in range(rank // high)], 0)
        q_out[:, cols] = q.astype(f32)
        full = jnp.dot(own2, jnp.concatenate([q, q], 0), preferred_element_type=f32)
        update[:, cols] = full.astype(bf16)
        side, at = divmod(l * wide, mine.shape[1])
        there = slice(at, at + wide)
        grad = jnp.where(c == side, mine[:, there].astype(f32), theirs[:, there].astype(f32))
        error_next[:, cols] = grad + err[:, cols] - full


def product_body(step, meta, a0, a1, y0, y1, out_a, out_b):
    c = meta[0]
    cols = y1.shape[1]
    count, rows, _ = out_a.shape
    lefts = []
    for a in (a0, a1):
        parts = []
        for d in range(2 * count):
            block = meta[2 + 2 * count * step + d]
            part = a[:, pl.ds(pl.multiple_of(block * rows, rows), rows)].T
            part = part.reshape(2, rows // 2, part.shape[1])
            parts += [jnp.where(c == 0, part[0], part[1]), jnp.where(c == 0, part[1], part[0])]
        lefts.append(jnp.concatenate(parts, 0))
    wide = 256
    for start in range(0, cols, wide):
        there = pl.ds(pl.multiple_of(c * cols, 128) + start, wide)
        total = jnp.dot(lefts[0], y0[:, there], preferred_element_type=f32)
        total += jnp.dot(lefts[1], y1[:, start : start + wide], preferred_element_type=f32)
        total = total.astype(bf16).reshape(2 * count, rows, wide)
        out_a[:, :, start : start + wide] = total[:count]
        out_b[:, :, start : start + wide] = total[count:]


def product(step, meta, a0, a1, y0, y1, side):
    tokens, dim = a0.shape
    cols = y1.shape[1]
    rows = dim // (side * side)
    out = shape((side // 2, rows, cols), bf16)
    ins = [(meta, SMEM), (a0, VMEM), (a1, VMEM), (y0, VMEM), (y1, VMEM)]
    return call(
        functools.partial(product_body, step), [out, out], ins,
        4 * tokens * side * rows * cols, "product" + str(step),
    )


def exchange(a, axes):
    return lax.all_to_all(a, axes, 0, 0, tiled=True)


def role(a, phase, step, side):
    def at(x, y, c):
        return (x % side * side + y % side) * 2 + c

    pairs = []
    for x in range(side):
        for y in range(side):
            for c in range(2):
                if (c == 0) == (phase == 1):
                    pairs.append((at(x, y, c), at(x + step, y, c)))
                else:
                    pairs.append((at(x, y, c), at(x, y + step, c)))
    return lax.ppermute(a, SHARD, pairs)


def add(*arrays):
    return sum(a.astype(f32) for a in arrays).astype(bf16)


def on_device(acts, cot, error_prev, q_prev):
    x, y, c = (lax.axis_index(name).astype(jnp.int32) for name in SHARD)
    n_rep = lax.axis_size("z")
    side = lax.axis_size("x")
    n_shard = side * side * 2
    swap = [(0, 1), (1, 0)]
    err = error_prev[0]
    own, ffw = err.shape
    rank = q_prev.shape[1]
    dim = acts.shape[1]
    half = ffw // 2

    first = jnp.arange(side * side, dtype=jnp.int32) // side
    second = jnp.arange(side * side, dtype=jnp.int32) % side
    to_x = (x + jnp.where(c == 0, first, second)) % side
    to_y = (y + jnp.where(c == 0, second, first)) % side
    meta = jnp.concatenate([jnp.stack([c, (x * side + y) * 2 + c]), to_x * side + to_y])

    acts_other = lax.ppermute(acts, "c", swap)
    cot_other = lax.ppermute(lax.dynamic_slice_in_dim(cot, (1 - c) * half, half, 1), "c", swap)

    high, wide = 8, rank * dim // n_shard // 8
    flops = 4 * rank * cot.size + 4 * rank * acts.size + 8 * rank * rank * ffw
    parts = call(
        left_body, [shape((n_shard, high, wide), f32)],
        [(meta, SMEM), (q_prev.T, VMEM), (cot, VMEM), (acts, VMEM), (err, VMEM)],
        flops, "left", [pltpu.VMEM((rank, dim), f32)],
    )[0]
    parts = exchange(parts, SHARD)
    parts = exchange(total(parts, n_rep, f32, "left_shard"), "z")
    parts = exchange(total(parts, n_shard, f32, "left_rep"), SHARD)

    mul = [product(step, meta, acts, acts_other, cot, cot_other, side) for step in (2, 1, 3, 0)]
    (g2a, g2b), (g1a, g1b), (g3a, g3b), (g0a, g0b) = mul
    from2a = role(g2a, 1, 1, side)
    from2b = role(g2b, 1, -1, side)
    from1b = role(g1b, 1, 1, side)
    from3a = role(g3a, 1, -1, side)
    from1a = role(add(g1a, from2a), 1, 1, side)
    from3b = role(add(g3b, from2b), 1, -1, side)
    ha = add(g0a, from1a, from3a)
    hb = add(g0b, from1b, from3b)
    near, far, back = role(ha[1], 2, 1, side), role(hb[0], 2, 2, side), role(hb[1], 2, -1, side)
    theirs = lax.ppermute(add(ha[0, own:], near[own:], far[own:], back[own:]), "c", swap)
    mine = add(ha[0, :own], near[:own], far[:own], back[:own])

    high, wide = 16, rank * ffw // n_shard // 16
    flops = 4 * rank * cot.size + 4 * rank * acts.size + 6 * rank * own * ffw + 30 * rank * rank * dim
    blocks, own_hat = call(
        right_body, [shape((n_shard, high, wide), bf16), shape((rank, own), f32)],
        [(meta, SMEM), (parts, VMEM), (acts, VMEM), (cot, VMEM), (err, VMEM)],
        flops, "right", [pltpu.VMEM((rank, dim), f32)],
    )
    blocks = exchange(blocks, SHARD)
    blocks = exchange(total(blocks, n_rep, f32, "right_shard"), "z")
    blocks = exchange(total(blocks, n_shard, bf16, "right_rep", 1.0 / n_rep), SHARD)

    update, error_next, q_t = call(
        last_body, [shape((own, ffw), bf16), shape((own, ffw), f32), shape((rank, ffw), f32)],
        [(meta, SMEM), (blocks, VMEM), (own_hat, VMEM), (mine, VMEM), (theirs, VMEM), (err, VMEM)],
        4 * own * rank * ffw, "last",
    )
    return update, error_next[None], q_t.T


def solution(mesh):
    reps, shards = mesh.devices.shape
    side = int((shards // 2) ** 0.5)
    grid = Mesh(mesh.devices.reshape(reps, side, side, 2), ("z",) + SHARD)
    every = ("z",) + SHARD
    return jax.shard_map(
        on_device,
        mesh=grid,
        in_specs=(P(every, None), P(every, None), P("z", SHARD, None), P()),
        out_specs=(P(SHARD, None), P("z", SHARD, None), P()),
        check_vma=False,
    )
```

```python
import functools

import jax
import jax.numpy as jnp
from jax import lax
from jax.experimental import pallas as pl
from jax.experimental.pallas import tpu as pltpu
from jax.sharding import Mesh, PartitionSpec as P

HI = lax.Precision.HIGHEST
SHARD = ("x", "y", "c")
f32 = jnp.float32
bf16 = jnp.bfloat16
VMEM = pl.BlockSpec(memory_space=pltpu.VMEM)
SMEM = pl.BlockSpec(memory_space=pltpu.SMEM)
HBM = pl.BlockSpec(memory_space=pl.ANY)
NT = (((1,), (1,)), ((), ()))
CHEAP = pl.CostEstimate(flops=1, bytes_accessed=1, transcendentals=0)
CHAIN = pl.CostEstimate(flops=5 * 10**10, bytes_accessed=1, transcendentals=0)
LARGE = 56 * 2**20


def terms(a, count):
    out = []
    for _ in range(count):
        top = a.astype(bf16)
        out.append(top)
        a = a - top.astype(f32)
    return out


def rows2(a):
    return jnp.concatenate(terms(a, 2), 0)


def fold(a):
    size = a.shape[0] // 2
    return a[:size] + a[size:]


def call(body, outs, ins, name, scratch=(), limit=8):
    return pl.pallas_call(
        body,
        out_shape=outs,
        in_specs=[spec for _, spec in ins],
        out_specs=[VMEM] * len(outs),
        scratch_shapes=list(scratch),
        name=name,
        compiler_params=pltpu.CompilerParams(vmem_limit_bytes=limit * 2**20),
        cost_estimate=CHAIN,
    )(*[a for a, _ in ins])


def shape(dims, dtype):
    return jax.ShapeDtypeStruct(dims, dtype)


def left_body(meta, q_t, cot, acts, err, out, t_sum, own_sum, p_t):
    step = pl.program_id(0)

    @pl.when(step == 0)
    def _():
        t_sum[...] = jnp.zeros_like(t_sum)
        own_sum[...] = jnp.zeros_like(own_sum)

    q2 = rows2(q_t[...])
    t_sum[...] += lax.dot_general(q2, cot[...], NT, preferred_element_type=f32)
    own_sum[...] += lax.dot_general(q2, rows2(err[...]), NT, preferred_element_type=f32)

    @pl.when(step == pl.num_programs(0) - 1)
    def _():
        p_t[...] = fold(jnp.dot(rows2(fold(t_sum[...])), acts[...], preferred_element_type=f32))
        rows = err.shape[0]
        own = fold(own_sum[...])
        own = own[:, :rows] + own[:, rows:]
        s = meta[1]
        zero = jnp.zeros_like(own)
        odd = (s % 2) == 1
        own = jnp.concatenate([jnp.where(odd, zero, own), jnp.where(odd, own, zero)], 1)
        at = pl.ds(pl.multiple_of((s // 2) * (2 * rows), 2 * rows), 2 * rows)
        p_t[:, at] += own
        _, high, wide = out.shape
        across = p_t.shape[1] // wide
        for block in range(out.shape[0]):
            g, l = divmod(block, across)
            out[block] = p_t[g * high : (g + 1) * high, l * wide : (l + 1) * wide]


def left(meta, q_t, cot, acts, err, n_shard):
    rank, ffw = q_t.shape
    tokens, dim = acts.shape
    rows = err.shape[0]
    chunk = ffw // 5
    high, wide = 8, rank * dim // n_shard // 8
    return pl.pallas_call(
        left_body,
        out_shape=shape((n_shard, high, wide), f32),
        grid_spec=pltpu.PrefetchScalarGridSpec(
            num_scalar_prefetch=1,
            grid=(ffw // chunk,),
            in_specs=[
                pl.BlockSpec((rank, chunk), lambda i, meta: (0, i)),
                pl.BlockSpec((tokens, chunk), lambda i, meta: (0, i)),
                pl.BlockSpec((tokens, dim), lambda i, meta: (0, 0)),
                pl.BlockSpec((rows, chunk), lambda i, meta: (0, i)),
            ],
            out_specs=pl.BlockSpec((n_shard, high, wide), lambda i, meta: (0, 0, 0)),
            scratch_shapes=[
                pltpu.VMEM((2 * rank, tokens), f32),
                pltpu.VMEM((2 * rank, 2 * rows), f32),
                pltpu.VMEM((rank, dim), f32),
            ],
        ),
        name="left",
        compiler_params=pltpu.CompilerParams(vmem_limit_bytes=LARGE),
        cost_estimate=CHAIN,
    )(meta, q_t, cot, acts, err)


def total_body(scale, part, out):
    total = part[0].astype(f32)
    for index in range(1, part.shape[0]):
        total += part[index].astype(f32)
    total = (total * scale).astype(out.dtype)
    for index in range(out.shape[0]):
        out[index] = total


def total(part, copies, dtype, name, scale=1.0):
    out = shape((copies,) + part.shape[1:], dtype)
    return call(functools.partial(total_body, scale), [out], [(part, VMEM)], name, limit=4)[0]


def inverse_factor(gram):
    n = gram.shape[0]
    ident = (
        lax.broadcasted_iota(jnp.int32, (n, n), 0) == lax.broadcasted_iota(jnp.int32, (n, n), 1)
    ).astype(f32)
    work = jnp.concatenate([gram, ident], 1)
    index = lax.broadcasted_iota(jnp.int32, work.shape, 0)
    step = 4
    for k in range(0, n, step):
        here = range(step)
        row = [work[k + i : k + i + 1, :] for i in here]
        col = [jnp.broadcast_to(work[:, k + i : k + i + 1], work.shape) for i in here]
        entry = [[col[j][k + i : k + i + 1, :] for j in here] for i in here]
        inv, root = [], []
        for j in here:
            inv.append(1.0 / entry[j][j])
            guess = lax.rsqrt(entry[j][j])
            root.append(guess * (1.5 - 0.5 * entry[j][j] * guess * guess))
            for i in range(j + 1, step):
                ratio = entry[i][j] * inv[j]
                row[i] = row[i] - ratio * row[j]
                for l in range(j + 1, step):
                    entry[i][l] = entry[i][l] - ratio * entry[j][l]
            for l in range(j + 1, step):
                col[l] = col[l] - col[j] * (inv[j] * entry[j][l])
        change = col[0] * (inv[0] * row[0])
        for j in range(1, step):
            change += col[j] * (inv[j] * row[j])
        work = jnp.where(index >= k + step, work - change, work)
        for j in here:
            work = jnp.where(index == k + j, row[j] * root[j], work)
    return work[:, n:]


def right_body(meta, parts, acts_hbm, cot_hbm, err_hbm, out, own_out, p_t, acts, cot, err, sems):
    pairs = ((acts_hbm, acts), (cot_hbm, cot), (err_hbm, err))
    copies = [pltpu.make_async_copy(a, b, sems.at[i]) for i, (a, b) in enumerate(pairs)]
    for copy in copies:
        copy.start()
    _, high, wide = parts.shape
    across = p_t.shape[1] // wide
    for block in range(parts.shape[0]):
        g, l = divmod(block, across)
        p_t[g * high : (g + 1) * high, l * wide : (l + 1) * wide] = parts[block]
    rank = p_t.shape[0]
    rows = err.shape[0]
    p = p_t[...]
    p3 = jnp.concatenate(terms(p, 3), 0)
    grams = lax.dot_general(p3, p3, NT, preferred_element_type=f32)
    gram = jnp.zeros((rank, rank), f32)
    for i in reversed(range(3)):
        for j in reversed(range(3)):
            gram += grams[i * rank : (i + 1) * rank, j * rank : (j + 1) * rank]
    inverse = inverse_factor(gram)
    p_hat = jnp.dot(inverse, p, precision=HI, preferred_element_type=f32)
    p_t[...] = p_hat
    copies[0].wait()
    w = fold(lax.dot_general(rows2(p_hat), acts[...], NT, preferred_element_type=f32))
    w2 = rows2(w)
    s = meta[1]
    both = p_t[:, pl.ds(pl.multiple_of((s // 2) * (2 * rows), 2 * rows), 2 * rows)]
    own = jnp.where((s % 2) == 1, both[:, rows:], both[:, :rows])
    own_out[...] = own
    own_top, own_rest = terms(own, 2)
    own3 = jnp.concatenate([own_top, own_rest, own_top], 1)
    copies[1].wait()
    copies[2].wait()
    _, high, wide = out.shape
    across = cot.shape[1] // wide
    for l in range(across):
        cols = slice(l * wide, (l + 1) * wide)
        err_top, err_rest = terms(err[:, cols], 2)
        err3 = jnp.concatenate([err_top, err_top, err_rest], 0)
        q = fold(jnp.dot(w2, cot[:, cols], preferred_element_type=f32))
        q += jnp.dot(own3, err3, preferred_element_type=f32)
        q = q.astype(out.dtype)
        for g in range(rank // high):
            out[g * across + l] = q[g * high : (g + 1) * high]


def last_body(meta, parts, own_t, mine, theirs, err, update, error_next, q_out):
    _, high, wide = parts.shape
    rank = own_t.shape[0]
    across = err.shape[1] // wide
    own_top, own_rest = terms(own_t[...].T, 2)
    own2 = jnp.concatenate([own_top, own_rest], 1)
    c = meta[0]
    for l in range(across):
        cols = slice(l * wide, (l + 1) * wide)
        q = jnp.concatenate([parts[g * across + l] for g in range(rank // high)], 0)
        q_out[:, cols] = q.astype(f32)
        full = jnp.dot(own2, jnp.concatenate([q, q], 0), preferred_element_type=f32)
        update[:, cols] = full.astype(bf16)
        side, at = divmod(l * wide, mine.shape[1])
        there = slice(at, at + wide)
        grad = jnp.where(c == side, mine[:, there].astype(f32), theirs[:, there].astype(f32))
        error_next[:, cols] = grad + err[:, cols] - full


def product_body(groups, side, meta, *refs):
    count = len(groups) * side
    lefts = refs[: 2 * count]
    y0, y1 = refs[2 * count : 2 * count + 2]
    outs = refs[2 * count + 2 : -1]
    left = refs[-1]
    rows = lefts[0].shape[1]
    c = meta[0]

    @pl.when(pl.program_id(0) == 0)
    def _():
        for i, ref in enumerate(lefts):
            part = ref[...].T
            one, two = part[: rows // 2], part[rows // 2 :]
            token, at = divmod(i, count)
            left[token, at * rows : at * rows + rows // 2] = jnp.where(c == 0, one, two)
            left[token, at * rows + rows // 2 : (at + 1) * rows] = jnp.where(c == 0, two, one)

    cols = y0.shape[1]
    wide = 256
    for start in range(0, cols, wide):
        there = slice(start, start + wide)
        full = jnp.dot(left[0], y0[:, there], preferred_element_type=f32)
        full += jnp.dot(left[1], y1[:, there], preferred_element_type=f32)
        full = full.astype(bf16).reshape(count, rows, wide)
        per = side // 2
        for i, out in enumerate(outs):
            out[:, :, there] = full[i * per : (i + 1) * per]


def product(groups, meta, a0, a1, y0, y1, side):
    tokens, dim = a0.shape
    cols = y1.shape[1] // 2
    rows = dim // (side * side)
    count = len(groups) * side
    chunk = 512
    steps = cols // chunk

    def block(place):
        return pl.BlockSpec((tokens, rows), lambda i, meta: (0, meta[2 + place]))

    places = [side * group + d for group in groups for d in range(side)]
    half = pl.BlockSpec((tokens, chunk), lambda i, meta: (0, meta[0] * steps + i))
    out = shape((side // 2, rows, cols), bf16)
    return pl.pallas_call(
        functools.partial(product_body, groups, side),
        out_shape=[out] * (2 * len(groups)),
        grid_spec=pltpu.PrefetchScalarGridSpec(
            num_scalar_prefetch=1,
            grid=(steps,),
            in_specs=[block(place) for place in places] * 2 + [half, half],
            out_specs=[pl.BlockSpec((side // 2, rows, chunk), lambda i, meta: (0, 0, i))]
            * (2 * len(groups)),
            scratch_shapes=[pltpu.VMEM((2, count * rows, tokens), bf16)],
        ),
        name="product" + str(groups[0]),
        compiler_params=pltpu.CompilerParams(vmem_limit_bytes=LARGE),
        cost_estimate=CHEAP,
    )(meta, *([a0] * count), *([a1] * count), y0, y1)


def after(a, *others):
    return lax.optimization_barrier((a,) + others)[0]


def exchange(a, axes):
    return lax.all_to_all(a, axes, 0, 0, tiled=True)


def role(a, phase, step, side):
    def at(x, y, c):
        return (x % side * side + y % side) * 2 + c

    pairs = []
    for x in range(side):
        for y in range(side):
            for c in range(2):
                if (c == 0) == (phase == 1):
                    pairs.append((at(x, y, c), at(x + step, y, c)))
                else:
                    pairs.append((at(x, y, c), at(x, y + step, c)))
    return lax.ppermute(a, SHARD, pairs)


def add(*arrays):
    return sum(a.astype(f32) for a in arrays).astype(bf16)


def on_device(acts, cot, error_prev, q_prev):
    x, y, c = (lax.axis_index(name).astype(jnp.int32) for name in SHARD)
    n_rep = lax.axis_size("z")
    side = lax.axis_size("x")
    n_shard = side * side * 2
    swap = [(0, 1), (1, 0)]
    err = error_prev[0]
    own, ffw = err.shape
    rank = q_prev.shape[1]
    dim = acts.shape[1]

    first = jnp.arange(side * side, dtype=jnp.int32) // side
    second = jnp.arange(side * side, dtype=jnp.int32) % side
    to_x = (x + jnp.where(c == 0, first, second)) % side
    to_y = (y + jnp.where(c == 0, second, first)) % side
    meta = jnp.concatenate([jnp.stack([c, (x * side + y) * 2 + c]), to_x * side + to_y])

    acts_other = lax.ppermute(acts, "c", swap)
    cot_other = lax.ppermute(cot, "c", swap)

    def piece(groups, token):
        return product(groups, after(meta, token), acts, acts_other, cot, cot_other, side)

    parts = left(meta, q_prev.T, cot, acts, err, n_shard)
    g2a, g2b, g1a, g1b = piece((2, 1), parts)
    from2a = role(g2a, 1, 1, side)
    from2b = role(g2b, 1, -1, side)
    from1b = role(g1b, 1, 1, side)
    parts = after(exchange(parts, SHARD), g2a)
    parts = total(parts, n_rep, f32, "left_shard")
    g3a, g3b, g0a, g0b = piece((3, 0), parts)
    from3a = role(g3a, 1, -1, side)
    from2a, from2b = after(from2a, parts), after(from2b, parts)
    parts = after(exchange(parts, "z"), g3a, from2a, from2b)
    parts = total(parts, n_shard, f32, "left_rep")
    g1a = add(g1a, after(from2a, parts))
    g3b = add(g3b, after(from2b, parts))
    from1a = role(g1a, 1, 1, side)
    from3b = role(g3b, 1, -1, side)
    parts = after(exchange(parts, SHARD), g1a, g3b)

    high, wide = 16, rank * ffw // n_shard // 16
    blocks, own_hat = call(
        right_body, [shape((n_shard, high, wide), bf16), shape((rank, own), f32)],
        [(meta, SMEM), (parts, VMEM), (acts, HBM), (cot, HBM), (err, HBM)],
        "right",
        [pltpu.VMEM((rank, dim), f32)]
        + [pltpu.VMEM(a.shape, a.dtype) for a in (acts, cot, err)]
        + [pltpu.SemaphoreType.DMA((3,))],
        limit=56,
    )
    from1a, from3a, from1b, from3b = (after(a, blocks) for a in (from1a, from3a, from1b, from3b))
    ha = add(g0a, from1a, from3a)
    hb = add(g0b, from1b, from3b)
    near, far, back = role(ha[1], 2, 1, side), role(hb[0], 2, 2, side), role(hb[1], 2, -1, side)
    blocks = after(exchange(blocks, SHARD), ha, hb)
    blocks = total(blocks, n_rep, bf16, "right_shard")
    near, far, back = (after(a, blocks) for a in (near, far, back))
    blocks = after(exchange(blocks, "z"), near, far, back)
    blocks = total(blocks, n_shard, bf16, "right_rep", 1.0 / n_rep)
    near, far, back = (after(a, blocks) for a in (near, far, back))
    theirs = lax.ppermute(add(ha[0, own:], near[own:], far[own:], back[own:]), "c", swap)
    mine = add(ha[0, :own], near[:own], far[:own], back[:own])
    blocks = exchange(blocks, SHARD)

    update, error_next, q_t = call(
        last_body, [shape((own, ffw), bf16), shape((own, ffw), f32), shape((rank, ffw), f32)],
        [(meta, SMEM), (blocks, VMEM), (own_hat, VMEM), (mine, VMEM), (theirs, VMEM), (err, VMEM)],
        "last", limit=8,
    )
    return update, error_next[None], q_t.T


def solution(mesh):
    reps, shards = mesh.devices.shape
    side = int((shards // 2) ** 0.5)
    grid = Mesh(mesh.devices.reshape(reps, side, side, 2), ("z",) + SHARD)
    every = ("z",) + SHARD
    return jax.shard_map(
        on_device,
        mesh=grid,
        in_specs=(P(every, None), P(every, None), P("z", SHARD, None), P()),
        out_specs=(P(SHARD, None), P("z", SHARD, None), P()),
        check_vma=False,
    )
```

```python
import functools

import jax
import jax.numpy as jnp
from jax import lax
from jax.experimental import pallas as pl
from jax.experimental.pallas import tpu as pltpu
from jax.sharding import Mesh, PartitionSpec as P

HI = lax.Precision.HIGHEST
SHARD = ("x", "y", "c")
f32 = jnp.float32
bf16 = jnp.bfloat16
VMEM = pl.BlockSpec(memory_space=pltpu.VMEM)
SMEM = pl.BlockSpec(memory_space=pltpu.SMEM)
HBM = pl.BlockSpec(memory_space=pl.ANY)
NT = (((1,), (1,)), ((), ()))
SHORT = pl.CostEstimate(flops=4 * 10**9, bytes_accessed=1, transcendentals=0)
CHEAP = pl.CostEstimate(flops=1, bytes_accessed=1, transcendentals=0)
CHAIN = pl.CostEstimate(flops=5 * 10**10, bytes_accessed=1, transcendentals=0)
LARGE = 56 * 2**20


def terms(a, count):
    out = []
    for _ in range(count):
        top = a.astype(bf16)
        out.append(top)
        a = a - top.astype(f32)
    return out


def rows2(a):
    return jnp.concatenate(terms(a, 2), 0)


def fold(a):
    size = a.shape[0] // 2
    return a[:size] + a[size:]


def call(body, outs, ins, name, scratch=(), limit=8, cost=CHAIN):
    return pl.pallas_call(
        body,
        out_shape=outs,
        in_specs=[spec for _, spec in ins],
        out_specs=[VMEM] * len(outs),
        scratch_shapes=list(scratch),
        name=name,
        compiler_params=pltpu.CompilerParams(vmem_limit_bytes=limit * 2**20),
        cost_estimate=cost,
    )(*[a for a, _ in ins])


def shape(dims, dtype):
    return jax.ShapeDtypeStruct(dims, dtype)


def left_body(meta, q_hbm, cot_hbm, acts_hbm, err_hbm, out, q_t, cot, acts, err, t, p_t, sems):
    tokens = cot.shape[0]
    chunks = sems.shape[0] - 3
    size = tokens // chunks
    slabs = [slice(i * size, (i + 1) * size) for i in range(chunks)]
    copies = [pltpu.make_async_copy(q_hbm, q_t, sems.at[chunks])]
    copies += [
        pltpu.make_async_copy(cot_hbm.at[slab], cot.at[slab], sems.at[i])
        for i, slab in enumerate(slabs)
    ]
    copies.append(pltpu.make_async_copy(acts_hbm, acts, sems.at[chunks + 1]))
    copies.append(pltpu.make_async_copy(err_hbm, err, sems.at[chunks + 2]))
    for copy in copies:
        copy.start()
    copies[0].wait()
    q2 = rows2(q_t[...])
    for copy, slab in zip(copies[1:-2], slabs):
        copy.wait()
        t[slab] = lax.dot_general(cot[slab], q2, NT, preferred_element_type=f32)
    t2 = rows2(fold(t[...].T))
    copies[-2].wait()
    p_t[...] = fold(jnp.dot(t2, acts[...], preferred_element_type=f32))
    copies[-1].wait()
    own = fold(lax.dot_general(q2, rows2(err[...]), NT, preferred_element_type=f32))
    rows = err.shape[0]
    own = own[:, :rows] + own[:, rows:]
    s = meta[0]
    zero = jnp.zeros_like(own)
    odd = (s % 2) == 1
    own = jnp.concatenate([jnp.where(odd, zero, own), jnp.where(odd, own, zero)], 1)
    at = pl.ds(pl.multiple_of((s // 2) * (2 * rows), 2 * rows), 2 * rows)
    p_t[:, at] += own
    _, high, wide = out.shape
    across = p_t.shape[1] // wide
    for block in range(out.shape[0]):
        g, l = divmod(block, across)
        out[block] = p_t[g * high : (g + 1) * high, l * wide : (l + 1) * wide]


def left(meta, q_t, cot, acts, err, n_shard):
    rank = q_t.shape[0]
    tokens, dim = acts.shape
    high, wide = 8, rank * dim // n_shard // 8
    return call(
        left_body, [shape((n_shard, high, wide), f32)],
        [(meta, SMEM), (q_t, HBM), (cot, HBM), (acts, HBM), (err, HBM)],
        "left",
        [pltpu.VMEM(a.shape, a.dtype) for a in (q_t, cot, acts, err)]
        + [pltpu.VMEM((tokens, 2 * rank), f32), pltpu.VMEM((rank, dim), f32)]
        + [pltpu.SemaphoreType.DMA((4 + 3,))],
        limit=56,
    )[0]


def total_body(scale, part, out):
    total = part[0].astype(f32)
    for index in range(1, part.shape[0]):
        total += part[index].astype(f32)
    total = (total * scale).astype(out.dtype)
    for index in range(out.shape[0]):
        out[index] = total


def total(part, copies, dtype, name, scale=1.0, cost=CHAIN):
    out = shape((copies,) + part.shape[1:], dtype)
    return call(functools.partial(total_body, scale), [out], [(part, VMEM)], name, limit=4, cost=cost)[0]


def inverse_factor(gram):
    n = gram.shape[0]
    ident = (
        lax.broadcasted_iota(jnp.int32, (n, n), 0) == lax.broadcasted_iota(jnp.int32, (n, n), 1)
    ).astype(f32)
    work = jnp.concatenate([gram, ident], 1)
    index = lax.broadcasted_iota(jnp.int32, work.shape, 0)
    step = 4
    for k in range(0, n, step):
        here = range(step)
        row = [work[k + i : k + i + 1, :] for i in here]
        col = [jnp.broadcast_to(work[:, k + i : k + i + 1], work.shape) for i in here]
        entry = [[col[j][k + i : k + i + 1, :] for j in here] for i in here]
        inv, root = [], []
        for j in here:
            inv.append(1.0 / entry[j][j])
            guess = lax.rsqrt(entry[j][j])
            root.append(guess * (1.5 - 0.5 * entry[j][j] * guess * guess))
            for i in range(j + 1, step):
                ratio = entry[i][j] * inv[j]
                row[i] = row[i] - ratio * row[j]
                for l in range(j + 1, step):
                    entry[i][l] = entry[i][l] - ratio * entry[j][l]
            for l in range(j + 1, step):
                col[l] = col[l] - col[j] * (inv[j] * entry[j][l])
        change = col[0] * (inv[0] * row[0])
        for j in range(1, step):
            change += col[j] * (inv[j] * row[j])
        work = jnp.where(index >= k + step, work - change, work)
        for j in here:
            work = jnp.where(index == k + j, row[j] * root[j], work)
    return work[:, n:]


def right_body(meta, parts, acts_hbm, cot_hbm, err_hbm, out, own_out, p_t, acts, cot, err, sems):
    pairs = ((acts_hbm, acts), (cot_hbm, cot), (err_hbm, err))
    copies = [pltpu.make_async_copy(a, b, sems.at[i]) for i, (a, b) in enumerate(pairs)]
    for copy in copies:
        copy.start()
    _, high, wide = parts.shape
    across = p_t.shape[1] // wide
    for block in range(parts.shape[0]):
        g, l = divmod(block, across)
        p_t[g * high : (g + 1) * high, l * wide : (l + 1) * wide] = parts[block]
    rank = p_t.shape[0]
    rows = err.shape[0]
    p = p_t[...]
    p3 = jnp.concatenate(terms(p, 3), 0)
    grams = lax.dot_general(p3, p3, NT, preferred_element_type=f32)
    gram = jnp.zeros((rank, rank), f32)
    for i in reversed(range(3)):
        for j in reversed(range(3)):
            gram += grams[i * rank : (i + 1) * rank, j * rank : (j + 1) * rank]
    inverse = inverse_factor(gram)
    p_hat = jnp.dot(inverse, p, precision=HI, preferred_element_type=f32)
    p_t[...] = p_hat
    copies[0].wait()
    w = fold(lax.dot_general(rows2(p_hat), acts[...], NT, preferred_element_type=f32))
    w2 = rows2(w)
    s = meta[1]
    both = p_t[:, pl.ds(pl.multiple_of((s // 2) * (2 * rows), 2 * rows), 2 * rows)]
    own = jnp.where((s % 2) == 1, both[:, rows:], both[:, :rows])
    own_out[...] = own
    own_top, own_rest = terms(own, 2)
    own3 = jnp.concatenate([own_top, own_rest, own_top], 1)
    copies[1].wait()
    copies[2].wait()
    _, high, wide = out.shape
    across = cot.shape[1] // wide
    for l in range(across):
        cols = slice(l * wide, (l + 1) * wide)
        err_top, err_rest = terms(err[:, cols], 2)
        err3 = jnp.concatenate([err_top, err_top, err_rest], 0)
        q = fold(jnp.dot(w2, cot[:, cols], preferred_element_type=f32))
        q += jnp.dot(own3, err3, preferred_element_type=f32)
        q = q.astype(out.dtype)
        for g in range(rank // high):
            out[g * across + l] = q[g * high : (g + 1) * high]


def last_body(meta, parts, own_t, mine, theirs, err, update, error_next, q_out):
    _, high, wide = parts.shape
    rank = own_t.shape[0]
    across = err.shape[1] // wide
    own_top, own_rest = terms(own_t[...].T, 2)
    own2 = jnp.concatenate([own_top, own_rest], 1)
    c = meta[0]
    for l in range(across):
        cols = slice(l * wide, (l + 1) * wide)
        q = jnp.concatenate([parts[g * across + l] for g in range(rank // high)], 0)
        q_out[:, cols] = q.astype(f32)
        full = jnp.dot(own2, jnp.concatenate([q, q], 0), preferred_element_type=f32)
        update[:, cols] = full.astype(bf16)
        side, at = divmod(l * wide, mine.shape[1])
        there = slice(at, at + wide)
        grad = jnp.where(c == side, mine[:, there].astype(f32), theirs[:, there].astype(f32))
        error_next[:, cols] = grad + err[:, cols] - full


def product_body(meta, a0, a1, y0, y1, *refs):
    outs, (a0_v, a1_v, left, right, full, sems, out_sems) = refs[:-7], refs[-7:]
    _, per, rows, cols = full.shape
    tokens = a0.shape[0]
    c = meta[0]
    at = pl.ds(pl.multiple_of(c * cols, 128), cols)
    copies = [
        pltpu.make_async_copy(a0, a0_v, sems.at[0]),
        pltpu.make_async_copy(a1, a1_v, sems.at[1]),
        pltpu.make_async_copy(y0.at[:, at], right.at[:tokens], sems.at[2]),
        pltpu.make_async_copy(y1.at[:, at], right.at[tokens:], sems.at[3]),
    ]
    for copy in copies:
        copy.start()
    copies[0].wait()
    copies[1].wait()
    wide = 512
    sent = []
    for step, out in enumerate(outs):
        for i in range(per):
            column = pl.ds(pl.multiple_of(meta[2 + per * step + i] * rows, rows), rows)
            for token, a in enumerate((a0_v, a1_v)):
                block = a[:, column].T
                one, two = block[: rows // 2], block[rows // 2 :]
                there = slice(token * tokens, (token + 1) * tokens)
                left[step, i * rows : i * rows + rows // 2, there] = jnp.where(c == 0, one, two)
                left[step, i * rows + rows // 2 : (i + 1) * rows, there] = jnp.where(c == 0, two, one)
        if step == 0:
            copies[2].wait()
            copies[3].wait()
        for start in range(0, cols, wide):
            there = slice(start, start + wide)
            total = jnp.dot(left[step], right[:, there], preferred_element_type=f32)
            full[step, :, :, there] = total.astype(bf16).reshape(per, rows, wide)
        sent.append(pltpu.make_async_copy(full.at[step], out, out_sems.at[step]))
        sent[-1].start()
    for copy in sent:
        copy.wait()


def product(meta, a0, a1, y0, y1, side):
    tokens, dim = a0.shape
    cols = y1.shape[1] // 2
    rows = dim // (side * side)
    steps = side * side // 2
    return pl.pallas_call(
        product_body,
        out_shape=[shape((2, rows, cols), bf16)] * steps,
        in_specs=[SMEM] + [HBM] * 4,
        out_specs=[HBM] * steps,
        scratch_shapes=[
            pltpu.VMEM((tokens, dim), bf16),
            pltpu.VMEM((tokens, dim), bf16),
            pltpu.VMEM((steps, 2 * rows, 2 * tokens), bf16),
            pltpu.VMEM((2 * tokens, cols), bf16),
            pltpu.VMEM((steps, 2, rows, cols), bf16),
            pltpu.SemaphoreType.DMA((4,)),
            pltpu.SemaphoreType.DMA((steps,)),
        ],
        name="product",
        compiler_params=pltpu.CompilerParams(vmem_limit_bytes=62 * 2**20),
        cost_estimate=CHEAP,
    )(meta, a0, a1, y0, y1)


def after(a, *others):
    return lax.optimization_barrier((a,) + others)[0]


def exchange(a, axes):
    return lax.all_to_all(a, axes, 0, 0, tiled=True)


def role(a, phase, step, side):
    def at(x, y, c):
        return (x % side * side + y % side) * 2 + c

    pairs = []
    for x in range(side):
        for y in range(side):
            for c in range(2):
                if (c == 0) == (phase == 1):
                    pairs.append((at(x, y, c), at(x + step, y, c)))
                else:
                    pairs.append((at(x, y, c), at(x, y + step, c)))
    return lax.ppermute(a, SHARD, pairs)


def add(*arrays):
    return sum(a.astype(f32) for a in arrays).astype(bf16)


def on_device(acts, cot, error_prev, q_prev):
    x, y, c = (lax.axis_index(name).astype(jnp.int32) for name in SHARD)
    n_rep = lax.axis_size("z")
    side = lax.axis_size("x")
    n_shard = side * side * 2
    swap = [(0, 1), (1, 0)]
    err = error_prev[0]
    own, ffw = err.shape
    rank = q_prev.shape[1]
    dim = acts.shape[1]

    order = [(2, 0), (2, 1), (2, 2), (2, 3), (1, 2), (1, 3), (3, 0), (3, 1)]
    order += [(1, 0), (1, 1), (3, 2), (3, 3), (0, 0), (0, 1), (0, 2), (0, 3)]
    first = jnp.array([place[0] for place in order], jnp.int32)
    second = jnp.array([place[1] for place in order], jnp.int32)
    to_x = (x + jnp.where(c == 0, first, second)) % side
    to_y = (y + jnp.where(c == 0, second, first)) % side
    s = (x * side + y) * 2 + c
    meta = jnp.concatenate([jnp.stack([c, s]), to_x * side + to_y])

    acts_other = lax.ppermute(acts, "c", swap)
    cot_other = lax.ppermute(cot, "c", swap)

    parts = left(s[None], q_prev.T, cot, acts, err, n_shard)
    g2a, g2b, g1b, g3a, g1a, g3b, g0a, g0b = product(
        after(meta, parts), acts, acts_other, cot, cot_other, side
    )
    parts = after(exchange(parts, SHARD), g0b)
    from2a = role(g2a, 1, 1, side)
    from2b = role(g2b, 1, -1, side)
    from1b = role(g1b, 1, 1, side)
    from3a = role(g3a, 1, -1, side)
    parts = total(parts, n_rep, f32, "left_shard")
    from2a, from2b = after(from2a, parts), after(from2b, parts)
    parts = after(exchange(parts, "z"), from2a, from2b)
    parts = total(parts, n_shard, f32, "left_rep")
    g1a = add(g1a, after(from2a, parts))
    g3b = add(g3b, after(from2b, parts))
    from1a = role(g1a, 1, 1, side)
    from3b = role(g3b, 1, -1, side)
    parts = after(exchange(parts, SHARD), g1a, g3b)

    high, wide = 16, rank * ffw // n_shard // 16
    blocks, own_hat = call(
        right_body, [shape((n_shard, high, wide), bf16), shape((rank, own), f32)],
        [(meta, SMEM), (parts, VMEM), (acts, HBM), (cot, HBM), (err, HBM)],
        "right",
        [pltpu.VMEM((rank, dim), f32)]
        + [pltpu.VMEM(a.shape, a.dtype) for a in (acts, cot, err)]
        + [pltpu.SemaphoreType.DMA((3,))],
        limit=56,
    )
    from1a, from3a, from1b, from3b = (after(a, blocks) for a in (from1a, from3a, from1b, from3b))
    ha = add(g0a, from1a, from3a)
    hb = add(g0b, from1b, from3b)
    near, far, back = role(ha[1], 2, 1, side), role(hb[0], 2, 2, side), role(hb[1], 2, -1, side)
    blocks = after(exchange(blocks, SHARD), ha, hb)
    blocks = total(blocks, n_rep, bf16, "right_shard", cost=SHORT)
    near, far, back = (after(a, blocks) for a in (near, far, back))
    blocks = after(exchange(blocks, "z"), near, far, back)
    blocks = total(blocks, n_shard, bf16, "right_rep", 1.0 / n_rep)
    near, far, back = (after(a, blocks) for a in (near, far, back))
    theirs = lax.ppermute(add(ha[0, own:], near[own:], far[own:], back[own:]), "c", swap)
    mine = add(ha[0, :own], near[:own], far[:own], back[:own])
    blocks = exchange(blocks, SHARD)

    update, error_next, q_t = call(
        last_body, [shape((own, ffw), bf16), shape((own, ffw), f32), shape((rank, ffw), f32)],
        [(meta, SMEM), (blocks, VMEM), (own_hat, VMEM), (mine, VMEM), (theirs, VMEM), (err, VMEM)],
        "last", limit=8,
    )
    return update, error_next[None], q_t.T


def solution(mesh):
    reps, shards = mesh.devices.shape
    side = int((shards // 2) ** 0.5)
    grid = Mesh(mesh.devices.reshape(reps, side, side, 2), ("z",) + SHARD)
    every = ("z",) + SHARD
    return jax.shard_map(
        on_device,
        mesh=grid,
        in_specs=(P(every, None), P(every, None), P("z", SHARD, None), P()),
        out_specs=(P(SHARD, None), P("z", SHARD, None), P()),
        check_vma=False,
    )
```

```python
import functools

import jax
import jax.numpy as jnp
from jax import lax
from jax.experimental import pallas as pl
from jax.experimental.pallas import tpu as pltpu
from jax.sharding import Mesh, PartitionSpec as P

HI = lax.Precision.HIGHEST
SHARD = ("x", "y", "c")
f32 = jnp.float32
bf16 = jnp.bfloat16
VMEM = pl.BlockSpec(memory_space=pltpu.VMEM)
SMEM = pl.BlockSpec(memory_space=pltpu.SMEM)
HBM = pl.BlockSpec(memory_space=pl.ANY)
NT = (((1,), (1,)), ((), ()))
CHEAP = pl.CostEstimate(flops=1, bytes_accessed=1, transcendentals=0)
CHAIN = pl.CostEstimate(flops=5 * 10**10, bytes_accessed=1, transcendentals=0)
LARGE = 56 * 2**20


def terms(a, count):
    out = []
    for _ in range(count):
        top = a.astype(bf16)
        out.append(top)
        a = a - top.astype(f32)
    return out


def rows2(a):
    return jnp.concatenate(terms(a, 2), 0)


def fold(a):
    size = a.shape[0] // 2
    return a[:size] + a[size:]


def call(body, outs, ins, name, scratch=(), limit=8, cost=CHAIN):
    return pl.pallas_call(
        body,
        out_shape=outs,
        in_specs=[spec for _, spec in ins],
        out_specs=[VMEM] * len(outs),
        scratch_shapes=list(scratch),
        name=name,
        compiler_params=pltpu.CompilerParams(vmem_limit_bytes=limit * 2**20),
        cost_estimate=cost,
    )(*[a for a, _ in ins])


def shape(dims, dtype):
    return jax.ShapeDtypeStruct(dims, dtype)


def left_body(meta, q_hbm, cot_hbm, acts_hbm, err_hbm, out, q_t, cot, acts, err, t, p_t, sems):
    tokens = cot.shape[0]
    chunks = sems.shape[0] - 3
    size = tokens // chunks
    slabs = [slice(i * size, (i + 1) * size) for i in range(chunks)]
    copies = [pltpu.make_async_copy(q_hbm, q_t, sems.at[chunks])]
    copies += [
        pltpu.make_async_copy(cot_hbm.at[slab], cot.at[slab], sems.at[i])
        for i, slab in enumerate(slabs)
    ]
    copies.append(pltpu.make_async_copy(acts_hbm, acts, sems.at[chunks + 1]))
    copies.append(pltpu.make_async_copy(err_hbm, err, sems.at[chunks + 2]))
    for copy in copies:
        copy.start()
    copies[0].wait()
    q2 = rows2(q_t[...])
    for copy, slab in zip(copies[1:-2], slabs):
        copy.wait()
        t[slab] = lax.dot_general(cot[slab], q2, NT, preferred_element_type=f32)
    t2 = rows2(fold(t[...].T))
    copies[-2].wait()
    p_t[...] = fold(jnp.dot(t2, acts[...], preferred_element_type=f32))
    copies[-1].wait()
    own = fold(lax.dot_general(q2, rows2(err[...]), NT, preferred_element_type=f32))
    rows = err.shape[0]
    own = own[:, :rows] + own[:, rows:]
    s = meta[0]
    zero = jnp.zeros_like(own)
    odd = (s % 2) == 1
    own = jnp.concatenate([jnp.where(odd, zero, own), jnp.where(odd, own, zero)], 1)
    at = pl.ds(pl.multiple_of((s // 2) * (2 * rows), 2 * rows), 2 * rows)
    p_t[:, at] += own
    _, high, wide = out.shape
    across = p_t.shape[1] // wide
    for block in range(out.shape[0]):
        g, l = divmod(block, across)
        out[block] = p_t[g * high : (g + 1) * high, l * wide : (l + 1) * wide]


def left(meta, q_t, cot, acts, err, n_shard):
    rank = q_t.shape[0]
    tokens, dim = acts.shape
    high, wide = 8, rank * dim // n_shard // 8
    return call(
        left_body, [shape((n_shard, high, wide), f32)],
        [(meta, SMEM), (q_t, HBM), (cot, HBM), (acts, HBM), (err, HBM)],
        "left",
        [pltpu.VMEM(a.shape, a.dtype) for a in (q_t, cot, acts, err)]
        + [pltpu.VMEM((tokens, 2 * rank), f32), pltpu.VMEM((rank, dim), f32)]
        + [pltpu.SemaphoreType.DMA((4 + 3,))],
        limit=56,
    )[0]


def total_body(scale, part, out):
    total = part[0].astype(f32)
    for index in range(1, part.shape[0]):
        total += part[index].astype(f32)
    total = (total * scale).astype(out.dtype)
    for index in range(out.shape[0]):
        out[index] = total


def total(part, copies, dtype, name, scale=1.0, cost=CHAIN):
    out = shape((copies,) + part.shape[1:], dtype)
    return call(functools.partial(total_body, scale), [out], [(part, VMEM)], name, limit=4, cost=cost)[0]


def inverse_factor(gram):
    n = gram.shape[0]
    ident = (
        lax.broadcasted_iota(jnp.int32, (n, n), 0) == lax.broadcasted_iota(jnp.int32, (n, n), 1)
    ).astype(f32)
    work = jnp.concatenate([gram, ident], 1)
    index = lax.broadcasted_iota(jnp.int32, work.shape, 0)
    step = 4
    for k in range(0, n, step):
        here = range(step)
        row = [work[k + i : k + i + 1, :] for i in here]
        col = [jnp.broadcast_to(work[:, k + i : k + i + 1], work.shape) for i in here]
        entry = [[col[j][k + i : k + i + 1, :] for j in here] for i in here]
        inv, root = [], []
        for j in here:
            inv.append(1.0 / entry[j][j])
            guess = lax.rsqrt(entry[j][j])
            root.append(guess * (1.5 - 0.5 * entry[j][j] * guess * guess))
            for i in range(j + 1, step):
                ratio = entry[i][j] * inv[j]
                row[i] = row[i] - ratio * row[j]
                for l in range(j + 1, step):
                    entry[i][l] = entry[i][l] - ratio * entry[j][l]
            for l in range(j + 1, step):
                col[l] = col[l] - col[j] * (inv[j] * entry[j][l])
        change = col[0] * (inv[0] * row[0])
        for j in range(1, step):
            change += col[j] * (inv[j] * row[j])
        work = jnp.where(index >= k + step, work - change, work)
        for j in here:
            work = jnp.where(index == k + j, row[j] * root[j], work)
    return work[:, n:]


def right_body(meta, parts, acts_hbm, cot_hbm, err_hbm, out, own_out, p_t, acts, cot, err, sems):
    pairs = ((acts_hbm, acts), (cot_hbm, cot), (err_hbm, err))
    copies = [pltpu.make_async_copy(a, b, sems.at[i]) for i, (a, b) in enumerate(pairs)]
    for copy in copies:
        copy.start()
    _, high, wide = parts.shape
    across = p_t.shape[1] // wide
    for block in range(parts.shape[0]):
        g, l = divmod(block, across)
        p_t[g * high : (g + 1) * high, l * wide : (l + 1) * wide] = parts[block]
    rank = p_t.shape[0]
    rows = err.shape[0]
    p = p_t[...]
    p3 = jnp.concatenate(terms(p, 3), 0)
    grams = lax.dot_general(p3, p3, NT, preferred_element_type=f32)
    gram = jnp.zeros((rank, rank), f32)
    for i in reversed(range(3)):
        for j in reversed(range(3)):
            gram += grams[i * rank : (i + 1) * rank, j * rank : (j + 1) * rank]
    inverse = inverse_factor(gram)
    p_hat = jnp.dot(inverse, p, precision=HI, preferred_element_type=f32)
    p_t[...] = p_hat
    copies[0].wait()
    w = fold(lax.dot_general(rows2(p_hat), acts[...], NT, preferred_element_type=f32))
    w2 = rows2(w)
    s = meta[0]
    both = p_t[:, pl.ds(pl.multiple_of((s // 2) * (2 * rows), 2 * rows), 2 * rows)]
    own = jnp.where((s % 2) == 1, both[:, rows:], both[:, :rows])
    own_out[...] = own
    own_top, own_rest = terms(own, 2)
    own3 = jnp.concatenate([own_top, own_rest, own_top], 1)
    copies[1].wait()
    copies[2].wait()
    _, high, wide = out.shape
    across = cot.shape[1] // wide
    for l in range(across):
        cols = slice(l * wide, (l + 1) * wide)
        err_top, err_rest = terms(err[:, cols], 2)
        err3 = jnp.concatenate([err_top, err_top, err_rest], 0)
        q = fold(jnp.dot(w2, cot[:, cols], preferred_element_type=f32))
        q += jnp.dot(own3, err3, preferred_element_type=f32)
        q = q.astype(out.dtype)
        for g in range(rank // high):
            out[g * across + l] = q[g * high : (g + 1) * high]


def last_body(meta, parts, own_t, mine, theirs, err, update, error_next, q_out):
    _, high, wide = parts.shape
    rank = own_t.shape[0]
    across = err.shape[1] // wide
    own_top, own_rest = terms(own_t[...].T, 2)
    own2 = jnp.concatenate([own_top, own_rest], 1)
    c = lax.rem(meta[0], jnp.int32(2))
    for l in range(across):
        cols = slice(l * wide, (l + 1) * wide)
        q = jnp.concatenate([parts[g * across + l] for g in range(rank // high)], 0)
        q_out[:, cols] = q.astype(f32)
        full = jnp.dot(own2, jnp.concatenate([q, q], 0), preferred_element_type=f32)
        update[:, cols] = full.astype(bf16)
        side, at = divmod(l * wide, mine.shape[1])
        there = slice(at, at + wide)
        grad = jnp.where(c == side, mine[:, there].astype(f32), theirs[:, there].astype(f32))
        error_next[:, cols] = grad + err[:, cols] - full


ORDER = [(2, 0), (2, 1), (2, 2), (2, 3), (1, 2), (1, 3), (3, 0), (3, 1)]
ORDER += [(1, 0), (1, 1), (3, 2), (3, 3), (0, 0), (0, 1), (0, 2), (0, 3)]


def place_of(s, side):
    two = jnp.int32(2)
    chip = lax.div(s, two)
    return lax.rem(s, two), lax.div(chip, jnp.int32(side)), lax.rem(chip, jnp.int32(side))


def product_body(side, meta, a0, a1, y0, y1, *refs):
    outs, (a0_v, a1_v, left, right, full, sems, out_sems) = refs[:-7], refs[-7:]
    _, per, rows, cols = full.shape
    tokens = a0.shape[0]
    c, x, y = place_of(meta[0], side)
    at = pl.ds(pl.multiple_of(c * cols, 128), cols)
    copies = [
        pltpu.make_async_copy(a0, a0_v, sems.at[0]),
        pltpu.make_async_copy(a1, a1_v, sems.at[1]),
        pltpu.make_async_copy(y0.at[:, at], right.at[:tokens], sems.at[2]),
        pltpu.make_async_copy(y1.at[:, at], right.at[tokens:], sems.at[3]),
    ]
    for copy in copies:
        copy.start()
    copies[0].wait()
    copies[1].wait()
    wide = 512
    sent = []
    for step, out in enumerate(outs):
        for i in range(per):
            first, second = ORDER[per * step + i]
            to_x = lax.rem(x + jnp.where(c == 0, first, second), jnp.int32(side))
            to_y = lax.rem(y + jnp.where(c == 0, second, first), jnp.int32(side))
            column = pl.ds(pl.multiple_of((to_x * side + to_y) * rows, rows), rows)
            for token, a in enumerate((a0_v, a1_v)):
                block = a[:, column].T
                one, two = block[: rows // 2], block[rows // 2 :]
                there = slice(token * tokens, (token + 1) * tokens)
                left[step, i * rows : i * rows + rows // 2, there] = jnp.where(c == 0, one, two)
                left[step, i * rows + rows // 2 : (i + 1) * rows, there] = jnp.where(c == 0, two, one)
        if step == 0:
            copies[2].wait()
            copies[3].wait()
        for start in range(0, cols, wide):
            there = slice(start, start + wide)
            total = jnp.dot(left[step], right[:, there], preferred_element_type=f32)
            full[step, :, :, there] = total.astype(bf16).reshape(per, rows, wide)
        sent.append(pltpu.make_async_copy(full.at[step], out, out_sems.at[step]))
        sent[-1].start()
    for copy in sent:
        copy.wait()


def product(meta, a0, a1, y0, y1, side):
    tokens, dim = a0.shape
    cols = y1.shape[1] // 2
    rows = dim // (side * side)
    steps = side * side // 2
    return pl.pallas_call(
        functools.partial(product_body, side),
        out_shape=[shape((2, rows, cols), bf16)] * steps,
        in_specs=[SMEM] + [HBM] * 4,
        out_specs=[HBM] * steps,
        scratch_shapes=[
            pltpu.VMEM((tokens, dim), bf16),
            pltpu.VMEM((tokens, dim), bf16),
            pltpu.VMEM((steps, 2 * rows, 2 * tokens), bf16),
            pltpu.VMEM((2 * tokens, cols), bf16),
            pltpu.VMEM((steps, 2, rows, cols), bf16),
            pltpu.SemaphoreType.DMA((4,)),
            pltpu.SemaphoreType.DMA((steps,)),
        ],
        name="product",
        compiler_params=pltpu.CompilerParams(vmem_limit_bytes=62 * 2**20),
        cost_estimate=CHEAP,
    )(meta, a0, a1, y0, y1)


def after(a, *others):
    return lax.optimization_barrier((a,) + others)[0]


def exchange(a, axes):
    return lax.all_to_all(a, axes, 0, 0, tiled=True)


def role(a, phase, step, side):
    def at(x, y, c):
        return (x % side * side + y % side) * 2 + c

    pairs = []
    for x in range(side):
        for y in range(side):
            for c in range(2):
                if (c == 0) == (phase == 1):
                    pairs.append((at(x, y, c), at(x + step, y, c)))
                else:
                    pairs.append((at(x, y, c), at(x, y + step, c)))
    return lax.ppermute(a, SHARD, pairs)


def add(*arrays):
    return sum(a.astype(f32) for a in arrays).astype(bf16)


def on_device(acts, cot, error_prev, q_prev):
    x, y, c = (lax.axis_index(name).astype(jnp.int32) for name in SHARD)
    n_rep = lax.axis_size("z")
    side = lax.axis_size("x")
    n_shard = side * side * 2
    swap = [(0, 1), (1, 0)]
    err = error_prev[0]
    own, ffw = err.shape
    rank = q_prev.shape[1]
    dim = acts.shape[1]

    meta = ((x * side + y) * 2 + c)[None]

    acts_other = lax.ppermute(acts, "c", swap)
    cot_other = lax.ppermute(cot, "c", swap)

    parts = left(meta, q_prev.T, cot, acts, err, n_shard)
    g2a, g2b, g1b, g3a, g1a, g3b, g0a, g0b = product(
        after(meta, parts), acts, acts_other, cot, cot_other, side
    )
    parts = after(exchange(parts, SHARD), g0b)
    from2a = role(g2a, 1, 1, side)
    from2b = role(g2b, 1, -1, side)
    from1b = role(g1b, 1, 1, side)
    from3a = role(g3a, 1, -1, side)
    parts = total(parts, n_rep, f32, "left_shard")
    from2a, from2b = after(from2a, parts), after(from2b, parts)
    parts = after(exchange(parts, "z"), from2a, from2b)
    parts = total(parts, n_shard, f32, "left_rep")
    g1a = add(g1a, after(from2a, parts))
    g3b = add(g3b, after(from2b, parts))
    from1a = role(g1a, 1, 1, side)
    from3b = role(g3b, 1, -1, side)
    parts = after(exchange(parts, SHARD), g1a, g3b)

    high, wide = 16, rank * ffw // n_shard // 16
    blocks, own_hat = call(
        right_body, [shape((n_shard, high, wide), bf16), shape((rank, own), f32)],
        [(meta, SMEM), (parts, VMEM), (acts, HBM), (cot, HBM), (err, HBM)],
        "right",
        [pltpu.VMEM((rank, dim), f32)]
        + [pltpu.VMEM(a.shape, a.dtype) for a in (acts, cot, err)]
        + [pltpu.SemaphoreType.DMA((3,))],
        limit=56,
    )
    from1a, from3a, from1b, from3b = (after(a, blocks) for a in (from1a, from3a, from1b, from3b))
    ha = add(g0a, from1a, from3a)
    hb = add(g0b, from1b, from3b)
    near, far, back = role(ha[1], 2, 1, side), role(hb[0], 2, 2, side), role(hb[1], 2, -1, side)
    blocks = after(exchange(blocks, SHARD), ha, hb)
    blocks = total(blocks, n_rep, bf16, "right_shard", cost=CHEAP)
    near, far, back = (after(a, blocks) for a in (near, far, back))
    blocks = after(exchange(blocks, "z"), near, far, back)
    blocks = total(blocks, n_shard, bf16, "right_rep", 1.0 / n_rep)
    near, far, back = (after(a, blocks) for a in (near, far, back))
    theirs = lax.ppermute(add(ha[0, own:], near[own:], far[own:], back[own:]), "c", swap)
    mine = add(ha[0, :own], near[:own], far[:own], back[:own])
    blocks = exchange(blocks, SHARD)

    update, error_next, q_t = call(
        last_body, [shape((own, ffw), bf16), shape((own, ffw), f32), shape((rank, ffw), f32)],
        [(meta, SMEM), (blocks, VMEM), (own_hat, VMEM), (mine, VMEM), (theirs, VMEM), (err, VMEM)],
        "last", limit=8,
    )
    return update, error_next[None], q_t.T


def solution(mesh):
    reps, shards = mesh.devices.shape
    side = int((shards // 2) ** 0.5)
    grid = Mesh(mesh.devices.reshape(reps, side, side, 2), ("z",) + SHARD)
    every = ("z",) + SHARD
    return jax.shard_map(
        on_device,
        mesh=grid,
        in_specs=(P(every, None), P(every, None), P("z", SHARD, None), P()),
        out_specs=(P(SHARD, None), P("z", SHARD, None), P()),
        check_vma=False,
    )
```

```python
import functools

import jax
import jax.numpy as jnp
from jax import lax
from jax.experimental import pallas as pl
from jax.experimental.pallas import tpu as pltpu
from jax.sharding import Mesh, PartitionSpec as P

HI = lax.Precision.HIGHEST
SHARD = ("x", "y", "c")
f32 = jnp.float32
bf16 = jnp.bfloat16
VMEM = pl.BlockSpec(memory_space=pltpu.VMEM)
SMEM = pl.BlockSpec(memory_space=pltpu.SMEM)
HBM = pl.BlockSpec(memory_space=pl.ANY)
NT = (((1,), (1,)), ((), ()))
CHEAP = pl.CostEstimate(flops=1, bytes_accessed=1, transcendentals=0)
CHAIN = pl.CostEstimate(flops=5 * 10**10, bytes_accessed=1, transcendentals=0)
LARGE = 56 * 2**20


def terms(a, count):
    out = []
    for _ in range(count):
        top = a.astype(bf16)
        out.append(top)
        a = a - top.astype(f32)
    return out


def rows2(a):
    return jnp.concatenate(terms(a, 2), 0)


def fold(a):
    size = a.shape[0] // 2
    return a[:size] + a[size:]


def call(body, outs, ins, name, scratch=(), limit=8, cost=CHAIN, place=VMEM):
    return pl.pallas_call(
        body,
        out_shape=outs,
        in_specs=[spec for _, spec in ins],
        out_specs=[place] * len(outs),
        scratch_shapes=list(scratch),
        name=name,
        compiler_params=pltpu.CompilerParams(vmem_limit_bytes=limit * 2**20),
        cost_estimate=cost,
    )(*[a for a, _ in ins])


def shape(dims, dtype):
    return jax.ShapeDtypeStruct(dims, dtype)


def left_body(meta, q_hbm, cot_hbm, acts_hbm, err_hbm, out, q_t, cot, acts, err, t, p_t, sems):
    tokens = cot.shape[0]
    chunks = sems.shape[0] - 3
    size = tokens // chunks
    slabs = [slice(i * size, (i + 1) * size) for i in range(chunks)]
    copies = [pltpu.make_async_copy(q_hbm, q_t, sems.at[chunks])]
    copies += [
        pltpu.make_async_copy(cot_hbm.at[slab], cot.at[slab], sems.at[i])
        for i, slab in enumerate(slabs)
    ]
    copies.append(pltpu.make_async_copy(acts_hbm, acts, sems.at[chunks + 1]))
    copies.append(pltpu.make_async_copy(err_hbm, err, sems.at[chunks + 2]))
    for copy in copies:
        copy.start()
    copies[0].wait()
    q2 = rows2(q_t[...])
    for copy, slab in zip(copies[1:-2], slabs):
        copy.wait()
        t[slab] = lax.dot_general(cot[slab], q2, NT, preferred_element_type=f32)
    t2 = rows2(fold(t[...].T))
    copies[-2].wait()
    p_t[...] = fold(jnp.dot(t2, acts[...], preferred_element_type=f32))
    copies[-1].wait()
    own = fold(lax.dot_general(q2, rows2(err[...]), NT, preferred_element_type=f32))
    rows = err.shape[0]
    own = own[:, :rows] + own[:, rows:]
    s = meta[0]
    zero = jnp.zeros_like(own)
    odd = (s % 2) == 1
    own = jnp.concatenate([jnp.where(odd, zero, own), jnp.where(odd, own, zero)], 1)
    at = pl.ds(pl.multiple_of((s // 2) * (2 * rows), 2 * rows), 2 * rows)
    p_t[:, at] += own
    _, high, wide = out.shape
    across = p_t.shape[1] // wide
    for block in range(out.shape[0]):
        g, l = divmod(block, across)
        out[block] = p_t[g * high : (g + 1) * high, l * wide : (l + 1) * wide]


def left(meta, q_t, cot, acts, err, n_shard):
    rank = q_t.shape[0]
    tokens, dim = acts.shape
    high, wide = 8, rank * dim // n_shard // 8
    return call(
        left_body, [shape((n_shard, high, wide), f32)],
        [(meta, SMEM), (q_t, HBM), (cot, HBM), (acts, HBM), (err, HBM)],
        "left",
        [pltpu.VMEM(a.shape, a.dtype) for a in (q_t, cot, acts, err)]
        + [pltpu.VMEM((tokens, 2 * rank), f32), pltpu.VMEM((rank, dim), f32)]
        + [pltpu.SemaphoreType.DMA((4 + 3,))],
        limit=56,
    )[0]


def total_body(scale, part, out):
    total = part[0].astype(f32)
    for index in range(1, part.shape[0]):
        total += part[index].astype(f32)
    total = (total * scale).astype(out.dtype)
    for index in range(out.shape[0]):
        out[index] = total


def total(part, copies, dtype, name, scale=1.0, cost=CHAIN):
    out = shape((copies,) + part.shape[1:], dtype)
    return call(functools.partial(total_body, scale), [out], [(part, VMEM)], name, limit=4, cost=cost)[0]


def inverse_factor(gram):
    n = gram.shape[0]
    ident = (
        lax.broadcasted_iota(jnp.int32, (n, n), 0) == lax.broadcasted_iota(jnp.int32, (n, n), 1)
    ).astype(f32)
    work = jnp.concatenate([gram, ident], 1)
    index = lax.broadcasted_iota(jnp.int32, work.shape, 0)
    step = 4
    for k in range(0, n, step):
        here = range(step)
        row = [work[k + i : k + i + 1, :] for i in here]
        col = [jnp.broadcast_to(work[:, k + i : k + i + 1], work.shape) for i in here]
        entry = [[col[j][k + i : k + i + 1, :] for j in here] for i in here]
        inv, root = [], []
        for j in here:
            inv.append(1.0 / entry[j][j])
            guess = lax.rsqrt(entry[j][j])
            root.append(guess * (1.5 - 0.5 * entry[j][j] * guess * guess))
            for i in range(j + 1, step):
                ratio = entry[i][j] * inv[j]
                row[i] = row[i] - ratio * row[j]
                for l in range(j + 1, step):
                    entry[i][l] = entry[i][l] - ratio * entry[j][l]
            for l in range(j + 1, step):
                col[l] = col[l] - col[j] * (inv[j] * entry[j][l])
        change = col[0] * (inv[0] * row[0])
        for j in range(1, step):
            change += col[j] * (inv[j] * row[j])
        work = jnp.where(index >= k + step, work - change, work)
        for j in here:
            work = jnp.where(index == k + j, row[j] * root[j], work)
    return work[:, n:]


def right_body(meta, parts, acts_hbm, cot_hbm, err_hbm, out, own_out, p_t, acts, cot, err, sems):
    pairs = ((acts_hbm, acts), (cot_hbm, cot), (err_hbm, err))
    copies = [pltpu.make_async_copy(a, b, sems.at[i]) for i, (a, b) in enumerate(pairs)]
    for copy in copies:
        copy.start()
    _, high, wide = parts.shape
    across = p_t.shape[1] // wide
    for block in range(parts.shape[0]):
        g, l = divmod(block, across)
        p_t[g * high : (g + 1) * high, l * wide : (l + 1) * wide] = parts[block]
    rank = p_t.shape[0]
    rows = err.shape[0]
    p = p_t[...]
    p3 = jnp.concatenate(terms(p, 3), 0)
    grams = lax.dot_general(p3, p3, NT, preferred_element_type=f32)
    gram = jnp.zeros((rank, rank), f32)
    for i in reversed(range(3)):
        for j in reversed(range(3)):
            gram += grams[i * rank : (i + 1) * rank, j * rank : (j + 1) * rank]
    inverse = inverse_factor(gram)
    p_hat = jnp.dot(inverse, p, precision=HI, preferred_element_type=f32)
    p_t[...] = p_hat
    copies[0].wait()
    w = fold(lax.dot_general(rows2(p_hat), acts[...], NT, preferred_element_type=f32))
    w2 = rows2(w)
    s = meta[0]
    both = p_t[:, pl.ds(pl.multiple_of((s // 2) * (2 * rows), 2 * rows), 2 * rows)]
    own = jnp.where((s % 2) == 1, both[:, rows:], both[:, :rows])
    own_out[...] = own
    own_top, own_rest = terms(own, 2)
    own3 = jnp.concatenate([own_top, own_rest, own_top], 1)
    copies[1].wait()
    copies[2].wait()
    _, high, wide = out.shape
    across = cot.shape[1] // wide
    for l in range(across):
        cols = slice(l * wide, (l + 1) * wide)
        err_top, err_rest = terms(err[:, cols], 2)
        err3 = jnp.concatenate([err_top, err_top, err_rest], 0)
        q = fold(jnp.dot(w2, cot[:, cols], preferred_element_type=f32))
        q += jnp.dot(own3, err3, preferred_element_type=f32)
        q = q.astype(out.dtype)
        for g in range(rank // high):
            out[g * across + l] = q[g * high : (g + 1) * high]


def last_body(meta, parts, own_t, mine, theirs, err, update_hbm, error_hbm, q_hbm, update, error_next, q_out, sems):
    sent = []
    _, high, wide = parts.shape
    rank = own_t.shape[0]
    across = err.shape[1] // wide
    own_top, own_rest = terms(own_t[...].T, 2)
    own2 = jnp.concatenate([own_top, own_rest], 1)
    c = lax.rem(meta[0], jnp.int32(2))
    for l in range(across):
        cols = slice(l * wide, (l + 1) * wide)
        q = jnp.concatenate([parts[g * across + l] for g in range(rank // high)], 0)
        q_out[:, cols] = q.astype(f32)
        full = jnp.dot(own2, jnp.concatenate([q, q], 0), preferred_element_type=f32)
        update[:, cols] = full.astype(bf16)
        side, at = divmod(l * wide, mine.shape[1])
        there = slice(at, at + wide)
        grad = jnp.where(c == side, mine[:, there].astype(f32), theirs[:, there].astype(f32))
        error_next[:, cols] = grad + err[:, cols] - full
        for a, to in ((update, update_hbm), (error_next, error_hbm), (q_out, q_hbm)):
            sent.append(pltpu.make_async_copy(a.at[:, cols], to.at[:, cols], sems.at[len(sent)]))
            sent[-1].start()
    for copy in sent:
        copy.wait()


ORDER = [(2, 0), (2, 1), (2, 2), (2, 3), (1, 2), (1, 3), (3, 0), (3, 1)]
ORDER += [(1, 0), (1, 1), (3, 2), (3, 3), (0, 0), (0, 1), (0, 2), (0, 3)]


def place_of(s, side):
    two = jnp.int32(2)
    chip = lax.div(s, two)
    return lax.rem(s, two), lax.div(chip, jnp.int32(side)), lax.rem(chip, jnp.int32(side))


def product_body(side, meta, a0, a1, y0, y1, *refs):
    outs, (soon, a0_v, a1_v, left, right, full, sems, soon_sems, out_sems) = refs[:-9], refs[-9:]
    _, per, rows, cols = full.shape
    tokens = a0.shape[0]
    c, x, y = place_of(meta[0], side)

    def column(n):
        first, second = ORDER[n]
        to_x = lax.rem(x + jnp.where(c == 0, first, second), jnp.int32(side))
        to_y = lax.rem(y + jnp.where(c == 0, second, first), jnp.int32(side))
        return pl.ds(pl.multiple_of((to_x * side + to_y) * rows, rows), rows)

    at = pl.ds(pl.multiple_of(c * cols, 128), cols)
    early = [
        pltpu.make_async_copy(a.at[:, column(i)], soon.at[2 * i + token], soon_sems.at[2 * i + token])
        for i in range(per)
        for token, a in enumerate((a0, a1))
    ]
    feed = [
        pltpu.make_async_copy(y0.at[:, at], right.at[:tokens], sems.at[0]),
        pltpu.make_async_copy(y1.at[:, at], right.at[tokens:], sems.at[1]),
    ]
    rest = [
        pltpu.make_async_copy(a0, a0_v, sems.at[2]),
        pltpu.make_async_copy(a1, a1_v, sems.at[3]),
    ]
    for copy in early + feed:
        copy.start()
    wide = 512
    sent = []
    for step, out in enumerate(outs):
        for copy in early if step == 0 else rest if step == 1 else []:
            copy.wait()
        for i in range(per):
            for token, a in enumerate((a0_v, a1_v)):
                block = (soon[2 * i + token] if step == 0 else a[:, column(per * step + i)]).T
                one, two = block[: rows // 2], block[rows // 2 :]
                there = slice(token * tokens, (token + 1) * tokens)
                left[step, i * rows : i * rows + rows // 2, there] = jnp.where(c == 0, one, two)
                left[step, i * rows + rows // 2 : (i + 1) * rows, there] = jnp.where(c == 0, two, one)
        if step == 0:
            for copy in feed:
                copy.wait()
            for copy in rest:
                copy.start()
        for start in range(0, cols, wide):
            there = slice(start, start + wide)
            total = jnp.dot(left[step], right[:, there], preferred_element_type=f32)
            full[step, :, :, there] = total.astype(bf16).reshape(per, rows, wide)
        sent.append(pltpu.make_async_copy(full.at[step], out, out_sems.at[step]))
        sent[-1].start()
    for copy in sent:
        copy.wait()


def product(meta, a0, a1, y0, y1, side):
    tokens, dim = a0.shape
    cols = y1.shape[1] // 2
    rows = dim // (side * side)
    steps = side * side // 2
    return pl.pallas_call(
        functools.partial(product_body, side),
        out_shape=[shape((2, rows, cols), bf16)] * steps,
        in_specs=[SMEM] + [HBM] * 4,
        out_specs=[HBM] * steps,
        scratch_shapes=[
            pltpu.VMEM((4, tokens, rows), bf16),
            pltpu.VMEM((tokens, dim), bf16),
            pltpu.VMEM((tokens, dim), bf16),
            pltpu.VMEM((steps, 2 * rows, 2 * tokens), bf16),
            pltpu.VMEM((2 * tokens, cols), bf16),
            pltpu.VMEM((steps, 2, rows, cols), bf16),
            pltpu.SemaphoreType.DMA((4,)),
            pltpu.SemaphoreType.DMA((4,)),
            pltpu.SemaphoreType.DMA((steps,)),
        ],
        name="product",
        compiler_params=pltpu.CompilerParams(vmem_limit_bytes=62 * 2**20),
        cost_estimate=CHEAP,
    )(meta, a0, a1, y0, y1)


def after(a, *others):
    return lax.optimization_barrier((a,) + others)[0]


def exchange(a, axes):
    return lax.all_to_all(a, axes, 0, 0, tiled=True)


def role(a, phase, step, side):
    def at(x, y, c):
        return (x % side * side + y % side) * 2 + c

    pairs = []
    for x in range(side):
        for y in range(side):
            for c in range(2):
                if (c == 0) == (phase == 1):
                    pairs.append((at(x, y, c), at(x + step, y, c)))
                else:
                    pairs.append((at(x, y, c), at(x, y + step, c)))
    return lax.ppermute(a, SHARD, pairs)


def add(*arrays):
    return sum(a.astype(f32) for a in arrays).astype(bf16)


def on_device(acts, cot, error_prev, q_prev):
    x, y, c = (lax.axis_index(name).astype(jnp.int32) for name in SHARD)
    n_rep = lax.axis_size("z")
    side = lax.axis_size("x")
    n_shard = side * side * 2
    swap = [(0, 1), (1, 0)]
    err = error_prev[0]
    own, ffw = err.shape
    rank = q_prev.shape[1]
    dim = acts.shape[1]

    meta = ((x * side + y) * 2 + c)[None]

    acts_other = lax.ppermute(acts, "c", swap)
    cot_other = lax.ppermute(cot, "c", swap)

    parts = left(meta, q_prev.T, cot, acts, err, n_shard)
    g2a, g2b, g1b, g3a, g1a, g3b, g0a, g0b = product(
        after(meta, parts), acts, acts_other, cot, cot_other, side
    )
    parts = after(exchange(parts, SHARD), g0b)
    from2a = role(g2a, 1, 1, side)
    from2b = role(g2b, 1, -1, side)
    from1b = role(g1b, 1, 1, side)
    from3a = role(g3a, 1, -1, side)
    parts = total(parts, n_rep, f32, "left_shard")
    from2a, from2b = after(from2a, parts), after(from2b, parts)
    parts = after(exchange(parts, "z"), from2a, from2b)
    parts = total(parts, n_shard, f32, "left_rep")
    g1a = add(g1a, after(from2a, parts))
    g3b = add(g3b, after(from2b, parts))
    from1a = role(g1a, 1, 1, side)
    from3b = role(g3b, 1, -1, side)
    parts = after(exchange(parts, SHARD), g1a, g3b)

    high, wide = 16, rank * ffw // n_shard // 16
    blocks, own_hat = call(
        right_body, [shape((n_shard, high, wide), bf16), shape((rank, own), f32)],
        [(meta, SMEM), (parts, VMEM), (acts, HBM), (cot, HBM), (err, HBM)],
        "right",
        [pltpu.VMEM((rank, dim), f32)]
        + [pltpu.VMEM(a.shape, a.dtype) for a in (acts, cot, err)]
        + [pltpu.SemaphoreType.DMA((3,))],
        limit=56,
    )
    from1a, from3a, from1b, from3b = (after(a, blocks) for a in (from1a, from3a, from1b, from3b))
    ha = add(g0a, from1a, from3a)
    hb = add(g0b, from1b, from3b)
    near, far, back = role(ha[1], 2, 1, side), role(hb[0], 2, 2, side), role(hb[1], 2, -1, side)
    blocks = after(exchange(blocks, SHARD), ha, hb)
    blocks = total(blocks, n_rep, bf16, "right_shard", cost=CHEAP)
    near, far, back = (after(a, blocks) for a in (near, far, back))
    blocks = after(exchange(blocks, "z"), near, far, back)
    blocks = total(blocks, n_shard, bf16, "right_rep", 1.0 / n_rep)
    near, far, back = (after(a, blocks) for a in (near, far, back))
    theirs = lax.ppermute(add(ha[0, own:], near[own:], far[own:], back[own:]), "c", swap)
    mine = add(ha[0, :own], near[:own], far[:own], back[:own])
    blocks = exchange(blocks, SHARD)

    outs = [shape((own, ffw), bf16), shape((own, ffw), f32), shape((rank, ffw), f32)]
    update, error_next, q_t = call(
        last_body, outs,
        [(meta, SMEM), (blocks, VMEM), (own_hat, VMEM), (mine, VMEM), (theirs, VMEM), (err, VMEM)],
        "last",
        [pltpu.VMEM(out.shape, out.dtype) for out in outs]
        + [pltpu.SemaphoreType.DMA((3 * n_shard * 16 // rank,))],
        limit=16, place=HBM,
    )
    return update, error_next[None], q_t.T


def solution(mesh):
    reps, shards = mesh.devices.shape
    side = int((shards // 2) ** 0.5)
    grid = Mesh(mesh.devices.reshape(reps, side, side, 2), ("z",) + SHARD)
    every = ("z",) + SHARD
    return jax.shard_map(
        on_device,
        mesh=grid,
        in_specs=(P(every, None), P(every, None), P("z", SHARD, None), P()),
        out_specs=(P(SHARD, None), P("z", SHARD, None), P()),
        check_vma=False,
    )
```
